32 devices in a mesh: dp: 4 (over z), row: 4 (over y, core), col: 2 (over x).
Axes of the slice: x: 2, y: 2, z: 4, core: 2. Of those that a mesh axis runs over, the one named last changes fastest.
Arguments:
- inputs: bfloat16 [8192, 1024], P(('dp', 'row'), 'col'), may hold values from -6 to 6
- cotangent: bfloat16 [8192, 1024], P(('dp', 'row'), 'col'), may hold values from -6 to 6
- norm_gain: float32 [1024], P('col'), may hold values from 0.5 to 1.5
- w_z: bfloat16 [1024, 1536], P('col', 'row'), may hold values from -0.1875 to 0.1875
- w_x: bfloat16 [1024, 1536], P('col', 'row'), may hold values from -0.1875 to 0.1875
- w_dt: bfloat16 [1024, 24], P('col', 'row'), may hold values from -0.09375 to 0.09375
- w_bc: bfloat16 [1024, 256], P('col'), may hold values from -0.1875 to 0.1875
- conv_x: bfloat16 [4, 1536], P(None, ('row', 'col')), may hold values from -3 to 3
- bias_x: float32 [1536], P(('row', 'col')), may hold values from -3 to 3
- conv_bc: bfloat16 [4, 256], replicated, may hold values from -3 to 3
- bias_bc: float32 [256], replicated, may hold values from -3 to 3
- dt_bias: float32 [24], P(('row', 'col')), may hold values from -4.5 to -2
- a_log: float32 [24], P(('row', 'col')), may hold values from 0 to 2.8
- d_skip: float32 [24], P(('row', 'col')), may hold values from 0.5 to 1.5
- mixer_gain: float32 [1536], P(('row', 'col')), may hold values from 0.5 to 1.5
- out_mamba: bfloat16 [1536, 1024], P('row', 'col'), may hold values from -0.15625 to 0.15625
- w_query: bfloat16 [1024, 512], P('col', 'row'), may hold values from -0.1875 to 0.1875
- key_matrix: bfloat16 [1024, 128], P('col'), may hold values from -0.1875 to 0.1875
- value_matrix: bfloat16 [1024, 128], P('col'), may hold values from -0.1875 to 0.1875
- out_attn: bfloat16 [512, 1024], P('row', 'col'), may hold values from -0.75 to 0.75
- ffn_gain: float32 [1024], P('col'), may hold values from 0.5 to 1.5
- w_gate: bfloat16 [1024, 2048], P('col', 'row'), may hold values from -0.1875 to 0.1875
- w_up: bfloat16 [1024, 2048], P('col', 'row'), may hold values from -0.1875 to 0.1875
- w_down: bfloat16 [2048, 1024], P('row', 'col'), may hold values from -0.125 to 0.125
Outputs:
- block_out: bfloat16 [8192, 1024], P(('dp', 'row'), 'col')
- grad_inputs: float32 [8192, 1024], P(('dp', 'row'), 'col')
- grad_norm_gain: float32 [1024], P('col')
- grad_w_z: float32 [1024, 1536], P('col', 'row')
- grad_w_x: float32 [1024, 1536], P('col', 'row')
- grad_w_dt: float32 [1024, 24], P('col', 'row')
- grad_w_bc: float32 [1024, 256], P('col')
- grad_conv_x: float32 [4, 1536], P(None, ('row', 'col'))
- grad_bias_x: float32 [1536], P(('row', 'col'))
- grad_conv_bc: float32 [4, 256], replicated
- grad_bias_bc: float32 [256], replicated
- grad_dt_bias: float32 [24], P(('row', 'col'))
- grad_a_log: float32 [24], P(('row', 'col'))
- grad_d_skip: float32 [24], P(('row', 'col'))
- grad_mixer_gain: float32 [1536], P(('row', 'col'))
- grad_out_mamba: float32 [1536, 1024], P('row', 'col')
- grad_w_query: float32 [1024, 512], P('col', 'row')
- key_weight_gradient: float32 [1024, 128], P('col')
- value_weight_gradient: float32 [1024, 128], P('col')
- grad_out_attn: float32 [512, 1024], P('row', 'col')
- grad_ffn_gain: float32 [1024], P('col')
- grad_w_gate: float32 [1024, 2048], P('col', 'row')
- grad_w_up: float32 [1024, 2048], P('col', 'row')
- grad_w_down: float32 [2048, 1024], P('row', 'col')
The draws below stay inside these ranges and needn't reach their ends.
All inputs are finite; a program needn't handle non-finite values.
Results may differ from the reference program's by a relative error of at most 0.035.
Values may be sent and summed in bfloat16 or wider, within the bound.
A program may use at most 128 MiB of HBM per device.

```python
import math
import jax
import jax.numpy as jnp
from jax import lax

MODEL_WIDTH = 1024
FF = 2048
MH = 24
STATE_SIZE = 128
KC = 4
QUERY_HEADS = 8
KEY_VALUE_HEADS = 2
HEAD_SIZE = 64
LEN = 2048
CH = 128
QB = 512
DM = 1536
TOKENS = 8192


def levels(stream_key, shape, cuts, low, top_value):
    factor_of = 1.0
    for axis_at, blocks in cuts:
        steps = jax.random.uniform(jax.random.fold_in(jax.random.fold_in(stream_key, 6), axis_at), (blocks,), jnp.float32, low / len(cuts), top_value / len(cuts))
        factor_of = factor_of * jnp.repeat(jnp.exp(steps), shape[axis_at] // blocks).reshape((-1,) + (1,) * (len(shape) - 1 - axis_at))
    return factor_of


def noise(stream_key, dims, deviation, reach, cuts=(), held_as=jnp.bfloat16):
    entries = deviation * jax.random.normal(stream_key, dims, jnp.float32)
    if cuts:
        entries = entries * levels(stream_key, dims, cuts, -0.22, 0.18)
    return jnp.clip(entries, -reach, reach).astype(held_as)


def setup_inputs(seed: int = 0) -> dict:
    key_list = jax.random.split(jax.random.key(seed), 25)
    return {
        "inputs": noise(key_list[0], (TOKENS, MODEL_WIDTH), 1.0, 6.0, ((0, 16), (1, 2))),
        "cotangent": noise(key_list[1], (TOKENS, MODEL_WIDTH), 1.0, 6.0, ((0, 16), (1, 2))),
        "norm_gain": jnp.clip(1.0 + 0.1 * jax.random.normal(key_list[2], (MODEL_WIDTH,), jnp.float32), 0.5, 1.5),
        "w_z": noise(key_list[3], (MODEL_WIDTH, DM), MODEL_WIDTH ** -0.5, 0.1875, ((0, 2), (1, 4))),
        "w_x": noise(key_list[4], (MODEL_WIDTH, DM), MODEL_WIDTH ** -0.5, 0.1875, ((0, 2), (1, 4))),
        "w_dt": noise(key_list[5], (MODEL_WIDTH, MH), (4 * MODEL_WIDTH) ** -0.5, 0.09375, ((0, 2), (1, 4))),
        "w_bc": noise(key_list[6], (MODEL_WIDTH, 2 * STATE_SIZE), MODEL_WIDTH ** -0.5, 0.1875, ((0, 2),)),
        "conv_x": noise(key_list[7], (KC, DM), KC ** -0.5, 3.0, ((1, 8),)),
        "bias_x": noise(key_list[8], (DM,), 0.5, 3.0, ((0, 8),), jnp.float32),
        "conv_bc": noise(key_list[9], (KC, 2 * STATE_SIZE), KC ** -0.5, 3.0),
        "bias_bc": noise(key_list[10], (2 * STATE_SIZE,), 0.5, 3.0, (), jnp.float32),
        "dt_bias": jnp.clip(-4.5 + 2.5 * jax.random.uniform(key_list[11], (MH,), jnp.float32) ** levels(key_list[11], (MH,), ((0, 8),), -0.2, 0.2), -4.5, -2.0),
        "a_log": jnp.clip(2.8 * jax.random.uniform(key_list[12], (MH,), jnp.float32) ** levels(key_list[12], (MH,), ((0, 8),), -0.2, 0.2), 0.0, 2.8),
        "d_skip": jnp.clip(0.5 + 1.0 * jax.random.uniform(key_list[13], (MH,), jnp.float32) ** levels(key_list[13], (MH,), ((0, 8),), -0.2, 0.2), 0.5, 1.5),
        "mixer_gain": jnp.clip(1.0 + 0.1 * jax.random.normal(key_list[14], (DM,), jnp.float32), 0.5, 1.5),
        "out_mamba": noise(key_list[15], (DM, MODEL_WIDTH), DM ** -0.5, 0.15625, ((0, 4), (1, 2))),
        "w_query": noise(key_list[16], (MODEL_WIDTH, QUERY_HEADS * HEAD_SIZE), MODEL_WIDTH ** -0.5, 0.1875, ((0, 2), (1, 4))),
        "key_matrix": noise(key_list[17], (MODEL_WIDTH, KEY_VALUE_HEADS * HEAD_SIZE), MODEL_WIDTH ** -0.5, 0.1875, ((0, 2),)),
        "value_matrix": noise(key_list[18], (MODEL_WIDTH, KEY_VALUE_HEADS * HEAD_SIZE), MODEL_WIDTH ** -0.5, 0.1875, ((0, 2),)),
        "out_attn": noise(key_list[19], (QUERY_HEADS * HEAD_SIZE, MODEL_WIDTH), HEAD_SIZE ** -0.5, 0.75, ((0, 4), (1, 2))),
        "ffn_gain": jnp.clip(1.0 + 0.1 * jax.random.normal(key_list[20], (MODEL_WIDTH,), jnp.float32), 0.5, 1.5),
        "w_gate": noise(key_list[21], (MODEL_WIDTH, FF), MODEL_WIDTH ** -0.5, 0.1875, ((0, 2), (1, 4))),
        "w_up": noise(key_list[22], (MODEL_WIDTH, FF), MODEL_WIDTH ** -0.5, 0.1875, ((0, 2), (1, 4))),
        "w_down": noise(key_list[23], (FF, MODEL_WIDTH), FF ** -0.5, 0.125, ((0, 4), (1, 2))),
    }


epsilon = 1e-05
rope_base = 100000000000.0
masked_score = -1e+30
highest = lax.Precision.HIGHEST

@jax.custom_vjp
def reduced_precision(v):
    return lax.optimization_barrier(v.astype(jnp.bfloat16)).astype(jnp.float32)

@jax.custom_vjp
def low_back(v):
    return v

def low_keep(v):
    return (reduced_precision(v), None)

def low_pass(kept, grad):
    return (grad,)

def back_keep(v):
    return (v, None)

def back_low(kept, grad):
    return (reduced_precision(grad),)
reduced_precision.defvjp(low_keep, low_pass)
low_back.defvjp(back_keep, back_low)

def rms_scale(values, gain):
    return values * lax.rsqrt(lax.optimization_barrier(jnp.mean(values * values, axis=-1, keepdims=True)) + epsilon) * gain

def causal_conv(raw, kernel, offset):
    sequence_length = raw.shape[0]
    padded = jnp.pad(raw, ((KC - 1, 0), (0, 0)))
    summed = offset + kernel[0] * padded[0:sequence_length]
    for tap_index in range(1, KC):
        summed = summed + kernel[tap_index] * padded[tap_index:tap_index + sequence_length]
    return jax.nn.silu(summed)

def apply_rotary(values, token_positions):
    half_width = values.shape[-1] // 2
    frequency = jnp.exp(jnp.arange(half_width).astype(jnp.float32) * (-2.0 * math.log(rope_base) / values.shape[-1]))
    angle_half = token_positions[:, None] * frequency[None, :]
    angle_full = jnp.concatenate([angle_half, angle_half], axis=-1)[:, None, :]
    turned = jnp.concatenate([-values[..., half_width:], values[..., :half_width]], axis=-1)
    return values * jnp.cos(angle_full) + turned * jnp.sin(angle_full)

def state_scan(values, b_rows, c_rows, step_sizes, log_decay):
    sequence_length, head_count, head_width = values.shape
    states = b_rows.shape[1]
    blocks = sequence_length // CH
    grouped = (values.reshape(blocks, CH, head_count, head_width), b_rows.reshape(blocks, CH, states), c_rows.reshape(blocks, CH, states), step_sizes.reshape(blocks, CH, head_count), log_decay.reshape(blocks, CH, head_count))
    position = jnp.arange(CH, dtype=jnp.int32)
    causal = (position[:, None] >= position[None, :])[:, :, None]

    def advance(carry_state, block_in):
        block_values, b_block, c_block, step_block, decay_block = block_in
        cumulative = jnp.cumsum(decay_block, axis=0)
        within = jnp.exp(jnp.where(causal, cumulative[:, None, :] - cumulative[None, :, :], masked_score))
        scores = jnp.dot(c_block, b_block.T, precision=highest)
        mixing = within * scores[:, :, None] * step_block[None, :, :]
        inside = jnp.einsum('ijh,jhp->ihp', mixing, block_values, precision=highest)
        carried = jnp.einsum('hpn,in->ihp', carry_state, c_block, precision=highest) * jnp.exp(cumulative)[:, :, None]
        tail_weight = jnp.exp(cumulative[-1][None, :] - cumulative) * step_block
        carry_state = jnp.exp(cumulative[-1])[:, None, None] * carry_state + jnp.einsum('jh,jhp,jn->hpn', tail_weight, block_values, b_block, precision=highest)
        return (carry_state, inside + carried)
    initial = jnp.zeros((head_count, head_width, states), values.dtype)
    _, outputs = lax.scan(jax.checkpoint(advance), initial, grouped)
    return outputs.reshape(sequence_length, head_count, head_width)

def mixer_core(conv_values, b_rows, c_rows, dt_raw, dt_bias, a_log, d_skip):
    sequence_length = conv_values.shape[0]
    head_count = dt_bias.shape[0]
    per_head = conv_values.reshape(sequence_length, head_count, -1)
    step_sizes = jax.nn.softplus(dt_raw + dt_bias)
    log_decay = -step_sizes * jnp.exp(a_log)
    output = state_scan(per_head, b_rows, c_rows, step_sizes, log_decay) + d_skip[:, None] * per_head
    return output.reshape(sequence_length, -1)

def attend(queries, key_rows, value_input):
    sequence_length = queries.shape[0]
    key_rows_gathered = jnp.repeat(key_rows, QUERY_HEADS // KEY_VALUE_HEADS, axis=1)
    value_rows_gathered = jnp.repeat(value_input, QUERY_HEADS // KEY_VALUE_HEADS, axis=1)
    key_pos = jnp.arange(sequence_length, dtype=jnp.int32)
    score_scale = HEAD_SIZE ** (-0.5)

    def block_out(first):
        query_blk = lax.dynamic_slice_in_dim(queries, first, QB, 0)
        scores = jnp.einsum('qhd,khd->hqk', query_blk, key_rows_gathered, precision=highest) * score_scale
        scores = low_back(scores)
        query_pos = first + jnp.arange(QB, dtype=jnp.int32)
        scores = jnp.where(key_pos[None, None, :] <= query_pos[None, :, None], scores, masked_score)
        weights = reduced_precision(jax.nn.softmax(scores, axis=-1))
        return jnp.einsum('hqk,khd->qhd', weights, value_rows_gathered, precision=highest)
    outputs = lax.map(jax.checkpoint(block_out), jnp.arange(sequence_length // QB, dtype=jnp.int32) * QB)
    return outputs.reshape(sequence_length, -1)

def layer(params, block_in):
    norm_gain, w_z, w_x, w_dt, w_bc, conv_x, bias_x, conv_bc, bias_bc, dt_bias, a_log, d_skip, mixer_gain, out_mamba, w_query, key_matrix, value_matrix, out_attn, ffn_gain, w_gate, w_up, w_down = params
    sequence_length = block_in.shape[0]
    normed = reduced_precision(rms_scale(block_in, norm_gain))

    def project(weight):
        return low_back(jnp.dot(normed, weight, precision=highest))
    gate_z = project(w_z)
    x_raw = project(w_x)
    dt_raw = project(w_dt)
    bc_raw = project(w_bc)
    q_raw = project(w_query)
    key_unrotated = project(key_matrix)
    value_unprojected = project(value_matrix)
    x_conv = reduced_precision(causal_conv(x_raw, conv_x, bias_x))
    bc_conv = reduced_precision(causal_conv(bc_raw, conv_bc, bias_bc))
    ssm_out = mixer_core(x_conv, bc_conv[:, :STATE_SIZE], bc_conv[:, STATE_SIZE:], dt_raw, dt_bias, a_log, d_skip)
    gated = ssm_out * jax.nn.silu(gate_z)
    mixed_low = reduced_precision(rms_scale(gated, mixer_gain))
    token_positions = jnp.arange(sequence_length).astype(jnp.float32)
    q_rot = reduced_precision(apply_rotary(q_raw.reshape(sequence_length, QUERY_HEADS, HEAD_SIZE), token_positions))
    key_rotated = reduced_precision(apply_rotary(key_unrotated.reshape(sequence_length, KEY_VALUE_HEADS, HEAD_SIZE), token_positions))
    value_reduced = reduced_precision(value_unprojected.reshape(sequence_length, KEY_VALUE_HEADS, HEAD_SIZE))
    attn_low = reduced_precision(low_back(attend(q_rot, key_rotated, value_reduced)))
    branch = low_back(jnp.dot(mixed_low, out_mamba, precision=highest) + jnp.dot(attn_low, out_attn, precision=highest))
    middle = block_in + branch
    normed_ffn = reduced_precision(rms_scale(middle, ffn_gain))
    gate_ffn = low_back(jnp.dot(normed_ffn, w_gate, precision=highest))
    up_ffn = low_back(jnp.dot(normed_ffn, w_up, precision=highest))
    act_low = reduced_precision(jax.nn.silu(gate_ffn) * up_ffn)
    return middle + low_back(jnp.dot(act_low, w_down, precision=highest))

def reference(inputs, cotangent, norm_gain, w_z, w_x, w_dt, w_bc, conv_x, bias_x, conv_bc, bias_bc, dt_bias, a_log, d_skip, mixer_gain, out_mamba, w_query, key_matrix, value_matrix, out_attn, ffn_gain, w_gate, w_up, w_down):
    params = tuple((array_in.astype(jnp.float32) for array_in in (norm_gain, w_z, w_x, w_dt, w_bc, conv_x, bias_x, conv_bc, bias_bc, dt_bias, a_log, d_skip, mixer_gain, out_mamba, w_query, key_matrix, value_matrix, out_attn, ffn_gain, w_gate, w_up, w_down)))
    seq_inputs = inputs.astype(jnp.float32).reshape(TOKENS // LEN, LEN, MODEL_WIDTH)
    seq_cots = cotangent.astype(jnp.float32).reshape(TOKENS // LEN, LEN, MODEL_WIDTH)

    def accumulate(sums, seq_pair):
        seq_in, seq_cot = seq_pair
        output, pullback = jax.vjp(layer, params, seq_in)
        grad_params, grad_in = pullback(seq_cot)
        return (jax.tree.map(jnp.add, sums, grad_params), (output.astype(jnp.bfloat16), grad_in))
    zeros = jax.tree.map(jnp.zeros_like, params)
    grads, (outputs, grad_ins) = lax.scan(accumulate, zeros, (seq_inputs, seq_cots))
    return (outputs.reshape(TOKENS, MODEL_WIDTH), grad_ins.reshape(TOKENS, MODEL_WIDTH), grads[0], grads[1], grads[2], grads[3], grads[4], grads[5], grads[6], grads[7], grads[8], grads[9], grads[10], grads[11], grads[12], grads[13], grads[14], grads[15], grads[16], grads[17], grads[18], grads[19], grads[20], grads[21])
```

```python
from functools import partial
import math

import jax
import jax.numpy as jnp
from jax import lax
from jax.experimental import pallas as pl
from jax.experimental.pallas import tpu as pltpu
from jax.sharding import PartitionSpec as P

MODEL_WIDTH = 1024
STATE_SIZE = 128
KC = 4
QUERY_HEADS = 8
KEY_VALUE_HEADS = 2
HEAD_SIZE = 64
CH = 128
QB = 512
DM = 1536


epsilon = 1e-05
rope_base = 100000000000.0
masked_score = -1e30
highest = lax.Precision.HIGHEST


def causal_conv(raw, kernel, offset):
    sequence_length = raw.shape[0]
    padded = jnp.pad(raw, ((KC - 1, 0), (0, 0)))
    summed = offset + kernel[0] * padded[0:sequence_length]
    for tap_index in range(1, KC):
        summed = summed + kernel[tap_index] * padded[tap_index : tap_index + sequence_length]
    return jax.nn.silu(summed)


def apply_rotary(values, token_positions):
    half_width = values.shape[-1] // 2
    frequency = jnp.exp(
        jnp.arange(half_width).astype(jnp.float32) * (-2.0 * math.log(rope_base) / values.shape[-1])
    )
    angle_half = token_positions[:, None] * frequency[None, :]
    angle_full = jnp.concatenate([angle_half, angle_half], axis=-1)[:, None, :]
    turned = jnp.concatenate([-values[..., half_width:], values[..., :half_width]], axis=-1)
    return values * jnp.cos(angle_full) + turned * jnp.sin(angle_full)


ROWS = ((1,), (1,))
COLS = ((0,), (0,))
VMEM_BYTES = 48 * 1024 * 1024


def dot_on(left, right, dims):
    return lax.dot_general(left, right, (dims, ((), ())), preferred_element_type=jnp.float32)


def chunk_masks():
    row = lax.broadcasted_iota(jnp.int32, (CH, CH), 0)
    column = lax.broadcasted_iota(jnp.int32, (CH, CH), 1)
    return row, column


def exact_dot(left, right, dims=((1,), (0,))):
    return lax.dot_general(
        left, right, (dims, ((), ())), precision=highest, preferred_element_type=jnp.float32
    )


def scan_forward_kernel(heads, x_ref, bc_ref, s_ref, a_ref, y_ref, start_ref, state):
    bf16 = jnp.bfloat16

    @pl.when(pl.program_id(0) == 0)
    def _():
        state[...] = jnp.zeros_like(state)

    carry = state[...]
    start_ref[0] = carry
    row, column = chunk_masks()
    causal = row >= column
    lower = jnp.where(causal, 1.0, 0.0)
    steps, decay = s_ref[...], a_ref[...]
    cum = exact_dot(lower, decay)
    cum_row = exact_dot(decay, lower, ((0,), (1,)))
    b_part, c_part = bc_ref[:, :STATE_SIZE], bc_ref[:, STATE_SIZE:]
    scores = dot_on(c_part, b_part, ROWS)
    carried = dot_on(c_part, carry.astype(bf16), ROWS)
    x_all = x_ref[...].astype(jnp.float32)
    width = x_all.shape[1] // heads
    outs, tails, ends = [], [], []
    for h in range(heads):
        span = slice(h * width, (h + 1) * width)
        c_h = cum[:, h : h + 1]
        last = cum[CH - 1 : CH, h : h + 1]
        xs = x_all[:, span] * steps[:, h : h + 1]
        within = jnp.exp(jnp.where(causal, c_h - cum_row[h : h + 1, :], masked_score))
        inside = jnp.dot(
            (within * scores).astype(bf16), xs.astype(bf16), preferred_element_type=jnp.float32
        )
        outs.append(inside + jnp.exp(c_h) * carried[:, span])
        tails.append((xs * jnp.exp(last - c_h)).astype(bf16))
        ends.append(jnp.exp(last))
    y_ref[...] = jnp.concatenate(outs, axis=1)
    update = dot_on(jnp.concatenate(tails, axis=1), b_part, COLS)
    for h in range(heads):
        span = slice(h * width, (h + 1) * width)
        state[span, :] = ends[h] * carry[span, :] + update[span, :]


def scan_backward_kernel(
    heads, x_ref, bc_ref, s_ref, a_ref, dy_ref, start_ref, dx_ref, ds_ref, da_ref, dbc_ref, dstate
):
    bf16 = jnp.bfloat16

    @pl.when(pl.program_id(0) == 0)
    def _():
        dstate[...] = jnp.zeros_like(dstate)

    dend = dstate[...]
    start = start_ref[0]
    dend_low, start_low = dend.astype(bf16), start.astype(bf16)
    row, column = chunk_masks()
    causal = row >= column
    strict = row > column
    lower = jnp.where(causal, 1.0, 0.0)
    upper = jnp.where(column >= row, 1.0, 0.0)
    upper_low = upper.astype(bf16)
    steps, decay = s_ref[...], a_ref[...]
    cum = exact_dot(lower, decay)
    cum_row = exact_dot(decay, lower, ((0,), (1,)))
    b_part, c_part = bc_ref[:, :STATE_SIZE], bc_ref[:, STATE_SIZE:]
    scores = dot_on(c_part, b_part, ROWS)
    carried = dot_on(c_part, start_low, ROWS)
    back = dot_on(b_part, dend_low, ROWS)
    x_all = x_ref[...].astype(jnp.float32)
    dy_all = dy_ref[...]
    dy_low = dy_all.astype(bf16)
    width = x_all.shape[1] // heads
    lane = lax.broadcasted_iota(jnp.int32, (CH, 8), 1)
    zero_small = jnp.zeros((CH, 8), jnp.float32)
    heads_q, heads_r, inner, ds_all = zero_small, zero_small, zero_small, zero_small
    dscores = jnp.zeros((CH, CH), jnp.float32)
    dxs_list, dye_list, tail_list, ends = [], [], [], []
    for h in range(heads):
        span = slice(h * width, (h + 1) * width)
        c_h = cum[:, h : h + 1]
        last = cum[CH - 1 : CH, h : h + 1]
        x_h = x_all[:, span]
        xs = x_h * steps[:, h : h + 1]
        dy_h = dy_all[:, span]
        e_cum = jnp.exp(c_h)
        tail = jnp.exp(last - c_h)
        within = jnp.exp(jnp.where(causal, c_h - cum_row[h : h + 1, :], masked_score))
        dmix = dot_on(dy_low[:, span], xs.astype(bf16), ROWS) * within
        dscores = dscores + dmix
        mixing = (within * scores).astype(bf16)
        back_h = tail * back[:, span]
        dxs = dot_on(mixing, dy_low[:, span], COLS) + back_h
        dye = dy_h * e_cum
        spread = jnp.dot(
            upper_low, (dmix * scores).astype(bf16), preferred_element_type=jnp.float32
        )
        end = jnp.exp(last)
        const = end * jnp.sum(
            jnp.sum(start[span, :] * dend[span, :], axis=1, keepdims=True), axis=0, keepdims=True
        )
        own = lane == h
        heads_q = jnp.where(own, jnp.sum(dye * carried[:, span], axis=1, keepdims=True), heads_q)
        heads_r = jnp.where(own, jnp.sum(xs * back_h, axis=1, keepdims=True), heads_r)
        inner = jnp.where(
            own, jnp.sum(jnp.where(strict, spread, 0.0), axis=1, keepdims=True) + const, inner
        )
        ds_all = jnp.where(own, jnp.sum(dxs * x_h, axis=1, keepdims=True), ds_all)
        dxs_list.append(dxs * steps[:, h : h + 1])
        dye_list.append(dye.astype(bf16))
        tail_list.append((xs * tail).astype(bf16))
        ends.append(end)
    dx_ref[...] = jnp.concatenate(dxs_list, axis=1)
    ds_ref[...] = ds_all
    da_ref[...] = (
        inner + exact_dot(upper, heads_q) + exact_dot(jnp.where(strict, 1.0, 0.0), heads_r)
    )
    dye_all = jnp.concatenate(dye_list, axis=1)
    dscores_low = dscores.astype(bf16)
    dbc_ref[:, :STATE_SIZE] = dot_on(dscores_low, c_part, COLS) + jnp.dot(
        jnp.concatenate(tail_list, axis=1), dend_low, preferred_element_type=jnp.float32
    )
    dbc_ref[:, STATE_SIZE:] = jnp.dot(
        dscores_low, b_part, preferred_element_type=jnp.float32
    ) + jnp.dot(dye_all, start_low, preferred_element_type=jnp.float32)
    update = dot_on(dye_all, c_part, COLS)
    for h in range(heads):
        span = slice(h * width, (h + 1) * width)
        dstate[span, :] = ends[h] * dend[span, :] + update[span, :]


def scan_forward(x_low, bc_low, steps, decay, heads):
    length, channels = x_low.shape
    chunks = length // CH
    rows = lambda width: pl.BlockSpec((CH, width), lambda i: (i, 0))
    return pl.pallas_call(
        partial(scan_forward_kernel, heads),
        grid=(chunks,),
        in_specs=[rows(channels), rows(2 * STATE_SIZE), rows(8), rows(8)],
        out_specs=[
            rows(channels),
            pl.BlockSpec((1, channels, STATE_SIZE), lambda i: (i, 0, 0)),
        ],
        out_shape=[
            jax.ShapeDtypeStruct((length, channels), jnp.float32),
            jax.ShapeDtypeStruct((chunks, channels, STATE_SIZE), jnp.float32),
        ],
        scratch_shapes=[pltpu.VMEM((channels, STATE_SIZE), jnp.float32)],
        compiler_params=pltpu.CompilerParams(vmem_limit_bytes=VMEM_BYTES),
        name="scan_forward",
    )(x_low, bc_low, steps, decay)


def scan_backward(x_low, bc_low, steps, decay, grad_out, starts, heads):
    length, channels = x_low.shape
    chunks = length // CH
    rows = lambda width: pl.BlockSpec((CH, width), lambda i: (chunks - 1 - i, 0))
    return pl.pallas_call(
        partial(scan_backward_kernel, heads),
        grid=(chunks,),
        in_specs=[
            rows(channels),
            rows(2 * STATE_SIZE),
            rows(8),
            rows(8),
            rows(channels),
            pl.BlockSpec((1, channels, STATE_SIZE), lambda i: (chunks - 1 - i, 0, 0)),
        ],
        out_specs=[rows(channels), rows(8), rows(8), rows(2 * STATE_SIZE)],
        out_shape=[
            jax.ShapeDtypeStruct((length, channels), jnp.float32),
            jax.ShapeDtypeStruct((length, 8), jnp.float32),
            jax.ShapeDtypeStruct((length, 8), jnp.float32),
            jax.ShapeDtypeStruct((length, 2 * STATE_SIZE), jnp.float32),
        ],
        scratch_shapes=[pltpu.VMEM((channels, STATE_SIZE), jnp.float32)],
        compiler_params=pltpu.CompilerParams(vmem_limit_bytes=VMEM_BYTES),
        name="scan_backward",
    )(x_low, bc_low, steps, decay, grad_out, starts)


AQ = 256


def masked_scores(q_blk, k_part, first):
    scores = dot_on(q_blk * jnp.bfloat16(HEAD_SIZE ** (-0.5)), k_part, ROWS)
    row = lax.broadcasted_iota(jnp.int32, scores.shape, 0) + first
    column = lax.broadcasted_iota(jnp.int32, scores.shape, 1)
    return jnp.where(column <= row, scores, masked_score)


def attend_forward_kernel(blocks, q_ref, k_ref, v_ref, o_ref, lse_ref):
    for index in range(blocks):

        @pl.when(pl.program_id(0) == index)
        def _(index=index):
            extent = (index + 1) * AQ
            scores = masked_scores(q_ref[...], k_ref[:extent, :], index * AQ)
            peak = jnp.max(scores, axis=1, keepdims=True)
            shifted = jnp.exp(scores - peak)
            total = jnp.sum(shifted, axis=1, keepdims=True)
            out = jnp.dot(
                shifted.astype(jnp.bfloat16), v_ref[:extent, :], preferred_element_type=jnp.float32
            )
            o_ref[...] = (out / total).astype(jnp.bfloat16)
            lse_ref[...] = peak + jnp.log(total)


def attend_backward_kernel(
    blocks, q_ref, k_ref, v_ref, g_ref, lse_ref, dq_ref, dk_ref, dv_ref
):
    scale = HEAD_SIZE ** (-0.5)

    @pl.when(pl.program_id(0) == 0)
    def _():
        dk_ref[...] = jnp.zeros_like(dk_ref)
        dv_ref[...] = jnp.zeros_like(dv_ref)

    for index in range(blocks):

        @pl.when(pl.program_id(0) == index)
        def _(index=index):
            extent = (index + 1) * AQ
            q_blk, g_blk = q_ref[...], g_ref[...]
            k_part, v_part = k_ref[:extent, :], v_ref[:extent, :]
            scores = masked_scores(q_blk, k_part, index * AQ)
            probs = jnp.exp(scores - lse_ref[...])
            grad_probs = dot_on(g_blk, v_part, ROWS)
            centre = jnp.sum(probs * grad_probs, axis=1, keepdims=True)
            grad_scores = (probs * (grad_probs - centre)).astype(jnp.bfloat16)
            dq_ref[...] = (
                jnp.dot(grad_scores, k_part, preferred_element_type=jnp.float32) * scale
            )
            dk_ref[:extent, :] += dot_on(grad_scores, q_blk, COLS) * scale
            dv_ref[:extent, :] += dot_on(probs.astype(jnp.bfloat16), g_blk, COLS)


def attend_forward(queries, key_rows, value_input):
    length = queries.shape[0]
    blocks = length // AQ
    whole = pl.BlockSpec((length, HEAD_SIZE), lambda i: (0, 0))
    part = lambda width: pl.BlockSpec((AQ, width), lambda i: (i, 0))
    return pl.pallas_call(
        partial(attend_forward_kernel, blocks),
        grid=(blocks,),
        in_specs=[part(HEAD_SIZE), whole, whole],
        out_specs=[part(HEAD_SIZE), part(1)],
        out_shape=[
            jax.ShapeDtypeStruct((length, HEAD_SIZE), jnp.bfloat16),
            jax.ShapeDtypeStruct((length, 1), jnp.float32),
        ],
        compiler_params=pltpu.CompilerParams(vmem_limit_bytes=VMEM_BYTES),
        name="attend_forward",
    )(queries, key_rows, value_input)


def attend_backward(queries, key_rows, value_input, grad_low, log_totals):
    length = queries.shape[0]
    blocks = length // AQ
    whole = pl.BlockSpec((length, HEAD_SIZE), lambda i: (0, 0))
    part = lambda width: pl.BlockSpec((AQ, width), lambda i: (i, 0))
    shape = jax.ShapeDtypeStruct((length, HEAD_SIZE), jnp.float32)
    return pl.pallas_call(
        partial(attend_backward_kernel, blocks),
        grid=(blocks,),
        in_specs=[part(HEAD_SIZE), whole, whole, part(HEAD_SIZE), part(1)],
        out_specs=[part(HEAD_SIZE), whole, whole],
        out_shape=[shape, shape, shape],
        compiler_params=pltpu.CompilerParams(vmem_limit_bytes=VMEM_BYTES),
        name="attend_backward",
    )(queries, key_rows, value_input, grad_low, log_totals)


def silu_slope(values):
    sigmoid = jax.nn.sigmoid(values)
    return sigmoid * (1.0 + values * (1.0 - sigmoid))


GRID = ("row", "col")


def swap(values):
    return lax.ppermute(values, "col", [(0, 1), (1, 0)])


def mine(values, axis):
    size = values.shape[axis] // lax.axis_size("col")
    return lax.dynamic_slice_in_dim(values, lax.axis_index("col") * size, size, axis)


def other(values, axis):
    size = values.shape[axis] // lax.axis_size("col")
    return lax.dynamic_slice_in_dim(values, (1 - lax.axis_index("col")) * size, size, axis)


def ordered(own, received, axis):
    first = lax.axis_index("col") == 0
    return jnp.concatenate(
        [jnp.where(first, own, received), jnp.where(first, received, own)], axis=axis
    )


def exchange(values, split_axis, join_axis):
    return ordered(mine(values, split_axis), swap(other(values, split_axis)), join_axis)


def gather_tokens(values):
    return lax.all_gather(values, GRID, axis=0, tiled=True)


def scatter_tokens(values):
    return lax.psum_scatter(
        values.astype(jnp.bfloat16), GRID, scatter_dimension=0, tiled=True
    ).astype(jnp.float32)


def grid_total(values):
    return lax.psum(values, GRID)


def norm_forward(values, gain):
    squares = jnp.sum(values * values, axis=-1)
    scale_row = lax.rsqrt(squares / MODEL_WIDTH + epsilon)
    return (values * scale_row[:, None] * gain, scale_row)


def norm_backward(values, scale_row, gain, grad_out):
    weighted = gain * grad_out
    inner_sum = jnp.sum(weighted * values, axis=-1)
    grad_in = (
        scale_row[:, None] * weighted - values * (scale_row**3 * inner_sum / MODEL_WIDTH)[:, None]
    )
    return (grad_in, jnp.sum(grad_out * values * scale_row[:, None], axis=0))


def dp_total(values):
    return lax.psum(values.astype(jnp.bfloat16), "dp")


def local(
    inputs,
    cotangent,
    norm_gain,
    w_z,
    w_x,
    w_dt,
    w_bc,
    conv_x,
    bias_x,
    conv_bc,
    bias_bc,
    dt_bias,
    a_log,
    d_skip,
    mixer_gain,
    out_mamba,
    w_query,
    key_matrix,
    value_matrix,
    out_attn,
    ffn_gain,
    w_gate,
    w_up,
    w_down,
):
    col_count = lax.axis_size("col")
    row_count = lax.axis_size("row")
    devices = col_count * row_count
    device_position = lax.axis_index("row") * col_count + lax.axis_index("col")
    sequence_length = inputs.shape[0] * row_count
    xw = conv_x.shape[1]
    heads = dt_bias.shape[0]
    ffn_local = w_down.shape[0] // col_count
    f32 = jnp.float32
    bf16 = jnp.bfloat16
    q_at, dt_at, s_at = 2 * xw, 2 * xw + HEAD_SIZE, 2 * xw + 2 * HEAD_SIZE

    x_float = exchange(inputs, 0, 1).astype(f32)
    pad = jnp.zeros((w_dt.shape[0], HEAD_SIZE - heads), bf16)
    sliced = [w_z, w_x, w_query, w_dt]
    shared = jnp.concatenate([w_bc, key_matrix, value_matrix], axis=1)
    own_in = jnp.concatenate([mine(w, 1) for w in sliced] + [pad, shared], axis=1)
    sent_in = jnp.concatenate([other(w, 1) for w in sliced] + [pad, shared], axis=1)
    w_all = ordered(own_in, swap(sent_in), 0)
    gains = jnp.stack([norm_gain, ffn_gain])
    gains = ordered(gains, swap(gains), 1)
    norm_gain, ffn_gain = gains[0], gains[1]
    key_value_head = device_position // (QUERY_HEADS // KEY_VALUE_HEADS)
    kv_at = s_at + 2 * STATE_SIZE
    key_at = kv_at + key_value_head * HEAD_SIZE
    value_at = key_at + KEY_VALUE_HEADS * HEAD_SIZE
    w_in = jnp.concatenate(
        [
            w_all[:, :kv_at],
            lax.dynamic_slice_in_dim(w_all, key_at, HEAD_SIZE, 1),
            lax.dynamic_slice_in_dim(w_all, value_at, HEAD_SIZE, 1),
        ],
        axis=1,
    )
    w_out = exchange(
        jnp.concatenate(
            [
                out_mamba.reshape(col_count, xw, -1),
                out_attn.reshape(col_count, HEAD_SIZE, -1),
                w_down.reshape(col_count, ffn_local, -1),
            ],
            axis=1,
        ).reshape(-1, out_mamba.shape[1]),
        0,
        1,
    )
    w_down_own = w_out[xw + HEAD_SIZE :]
    w_out = w_out[: xw + HEAD_SIZE]
    w_ffn = jnp.concatenate([mine(w_gate, 1), mine(w_up, 1)], axis=1)
    w_ffn = ordered(w_ffn, swap(jnp.concatenate([other(w_gate, 1), other(w_up, 1)], axis=1)), 0)
    cot_own = exchange(cotangent, 0, 1)

    normed, scale_one = norm_forward(x_float, norm_gain)
    normed_all = gather_tokens(normed.astype(bf16))
    cot_all = gather_tokens(cot_own)
    projected = jnp.dot(normed_all, w_in, preferred_element_type=f32)
    gate_z = projected[:, :xw]
    x_raw = projected[:, xw : 2 * xw]
    q_raw = projected[:, q_at:dt_at]
    dt_raw = projected[:, dt_at : dt_at + heads]
    bc_raw = projected[:, s_at:kv_at]
    key_unrotated = projected[:, kv_at : kv_at + HEAD_SIZE]
    value_reduced = projected[:, kv_at + HEAD_SIZE :].astype(bf16)
    x_conv, x_conv_pull = jax.vjp(causal_conv, x_raw, conv_x.astype(f32), bias_x)
    bc_conv, bc_conv_pull = jax.vjp(causal_conv, bc_raw, conv_bc.astype(f32), bias_bc)
    x_low = x_conv.astype(bf16)
    bc_low = bc_conv.astype(bf16)
    steps = jax.nn.softplus(dt_raw + dt_bias)
    log_decay = -steps * jnp.exp(a_log)
    widen = ((0, 0), (0, 8 - heads))
    steps_wide, decay_wide = jnp.pad(steps, widen), jnp.pad(log_decay, widen)
    scanned, starts = scan_forward(x_low, bc_low, steps_wide, decay_wide, heads)
    head_width = xw // heads
    skip_row = jnp.repeat(d_skip, head_width)
    ssm_out = scanned + skip_row * x_low.astype(f32)
    gated = ssm_out * jax.nn.silu(gate_z)
    mixer_scale = lax.rsqrt(grid_total(jnp.sum(gated * gated, axis=-1)) / DM + epsilon)
    mixed_low = (gated * mixer_scale[:, None] * mixer_gain).astype(bf16)
    token_positions = jnp.arange(sequence_length).astype(f32)
    qk_rot, qk_pull = jax.vjp(
        partial(apply_rotary, token_positions=token_positions),
        jnp.stack([q_raw, key_unrotated], axis=1),
    )
    q_low = qk_rot[:, 0].astype(bf16)
    k_low = qk_rot[:, 1].astype(bf16)
    attn_low, log_totals = attend_forward(q_low, k_low, value_reduced)
    joined = jnp.concatenate([mixed_low, attn_low], axis=1)
    middle = x_float + scatter_tokens(jnp.dot(joined, w_out, preferred_element_type=f32))
    normed_ffn, scale_two = norm_forward(middle, ffn_gain)
    ffn_all = gather_tokens(normed_ffn.astype(bf16))
    gate_up = jnp.dot(ffn_all, w_ffn, preferred_element_type=f32)
    gate_ffn = gate_up[:, :ffn_local]
    up_ffn = gate_up[:, ffn_local:]
    gate_silu = jax.nn.silu(gate_ffn)
    act = (gate_silu * up_ffn).astype(bf16)
    grad_act = dot_on(cot_all, w_down_own, ROWS)
    grad_gate = grad_act * up_ffn * silu_slope(gate_ffn)
    grad_up = grad_act * gate_silu
    grad_ffn = jnp.concatenate([grad_gate, grad_up], axis=1).astype(bf16)
    grad_ffn_in = scatter_tokens(dot_on(grad_ffn, w_ffn, ROWS))
    block_out = middle + scatter_tokens(jnp.dot(act, w_down_own, preferred_element_type=f32))
    block_out = exchange(block_out.astype(bf16), 1, 0)
    grad_w_ffn = dp_total(dot_on(ffn_all, grad_ffn, COLS))
    grad_w_down = dp_total(dot_on(act, cot_all, COLS))
    grad_middle_norm, grad_ffn_gain = norm_backward(middle, scale_two, ffn_gain, grad_ffn_in)
    grad_middle = cot_own.astype(f32) + grad_middle_norm
    grad_branch_all = gather_tokens(grad_middle.astype(bf16))
    grad_w_out = dp_total(dot_on(joined, grad_branch_all, COLS))
    grad_joined = dot_on(grad_branch_all, w_out, ROWS)
    grad_mixed = grad_joined[:, :xw]
    grad_attn = grad_joined[:, xw:].astype(bf16)
    weighted = mixer_gain * grad_mixed
    inner_sum = grid_total(jnp.sum(weighted * gated, axis=-1))
    grad_q_rot, grad_k_rot, value_gradient = attend_backward(
        q_low, k_low, value_reduced, grad_attn, log_totals
    )
    grad_qk = qk_pull(jnp.stack([grad_q_rot, grad_k_rot], axis=1))[0]
    grad_gated = (
        mixer_scale[:, None] * weighted - gated * (mixer_scale**3 * inner_sum / DM)[:, None]
    )
    grad_mixer_gain = jnp.sum(grad_mixed * gated * mixer_scale[:, None], axis=0)
    grad_ssm = grad_gated * jax.nn.silu(gate_z)
    grad_z = grad_gated * ssm_out * silu_slope(gate_z)
    grad_x_scan, grad_steps, grad_decay, grad_bc = scan_backward(
        x_low, bc_low, steps_wide, decay_wide, grad_ssm, starts, heads
    )
    grad_xc = grad_x_scan + skip_row * grad_ssm
    grad_d_skip = jnp.sum(
        jnp.sum(grad_ssm * x_low.astype(f32), axis=0).reshape(heads, head_width), axis=1
    )
    grad_decay = grad_decay[:, :heads]
    grad_dt = (grad_steps[:, :heads] - grad_decay * jnp.exp(a_log)) * jax.nn.sigmoid(
        dt_raw + dt_bias
    )
    grad_dt_bias = jnp.sum(grad_dt, axis=0)
    grad_a_log = jnp.sum(grad_decay * log_decay, axis=0)
    grad_x_raw, grad_conv_x, grad_bias_x = x_conv_pull(grad_xc)
    grad_bc_raw, grad_conv_bc, grad_bias_bc = bc_conv_pull(grad_bc)
    grad_in = jnp.concatenate(
        [
            grad_z,
            grad_x_raw,
            grad_qk[:, 0],
            grad_dt,
            jnp.zeros((sequence_length, HEAD_SIZE - heads), f32),
            grad_bc_raw,
            grad_qk[:, 1],
            value_gradient,
        ],
        axis=1,
    ).astype(bf16)
    grad_normed = scatter_tokens(dot_on(grad_in, w_in, ROWS))
    grad_w_in = dot_on(normed_all, grad_in, COLS)
    head_selection = (jnp.arange(KEY_VALUE_HEADS) == key_value_head).astype(f32)

    def per_head(values):
        return (head_selection[None, :, None] * values[:, None, :]).reshape(values.shape[0], -1)

    grad_w_shared = jnp.concatenate(
        [
            grad_w_in[:, s_at:kv_at],
            per_head(grad_w_in[:, kv_at : kv_at + HEAD_SIZE]),
            per_head(grad_w_in[:, kv_at + HEAD_SIZE :]),
        ],
        axis=1,
    )
    grad_w_shared = lax.psum_scatter(
        grad_w_shared.astype(bf16), ("col", "row"), scatter_dimension=0, tiled=True
    )
    grad_w_main = dp_total(grad_w_in[:, :s_at])
    grad_w_shared = lax.all_gather(lax.psum(grad_w_shared, "dp"), "row", axis=0, tiled=True)
    grad_x_norm, grad_norm_gain = norm_backward(x_float, scale_one, norm_gain, grad_normed)
    grad_inputs = exchange((grad_middle + grad_x_norm).astype(bf16), 1, 0).astype(f32)

    slot = jnp.concatenate(
        [
            grad_conv_x.reshape(-1),
            grad_bias_x,
            grad_mixer_gain,
            grad_dt_bias,
            grad_a_log,
            grad_d_skip,
        ]
    )
    common = jnp.concatenate(
        [grad_conv_bc.reshape(-1), grad_bias_bc, grad_norm_gain, grad_ffn_gain]
    )
    chosen = (jnp.arange(devices) == device_position).astype(f32)
    small = jnp.concatenate([common, (chosen[:, None] * slot[None, :]).reshape(-1)])
    small = lax.psum(small, ("dp", "row", "col"))
    common_size, slot_size = common.shape[0], slot.shape[0]
    slot = lax.dynamic_slice_in_dim(small, common_size + device_position * slot_size, slot_size, 0)
    conv_end = KC * xw
    grad_conv_x = slot[:conv_end].reshape(KC, xw)
    grad_bias_x = slot[conv_end : conv_end + xw]
    grad_mixer_gain = slot[conv_end + xw : conv_end + 2 * xw]
    tail = slot[conv_end + 2 * xw :]
    grad_dt_bias, grad_a_log, grad_d_skip = tail[:heads], tail[heads : 2 * heads], tail[2 * heads :]
    shared_width = 2 * STATE_SIZE
    grad_conv_bc = small[: KC * shared_width].reshape(KC, shared_width)
    at = KC * shared_width
    grad_bias_bc = small[at : at + shared_width]
    at = at + shared_width
    grad_norm_gain = mine(small[at : at + MODEL_WIDTH], 0)
    grad_ffn_gain = mine(small[at + MODEL_WIDTH : at + 2 * MODEL_WIDTH], 0)

    def back(values, axis):
        own, received = mine(values, axis), swap(other(values, axis))
        first = lax.axis_index("col") == 0
        left = jnp.where(first, own, received).astype(f32)
        right = jnp.where(first, received, own).astype(f32)

        def part(start, size, along):
            return jnp.concatenate(
                [lax.slice_in_dim(v, start, start + size, axis=along) for v in (left, right)],
                axis=along,
            )

        return part

    main_part = back(grad_w_main, 0)
    grad_w_z = main_part(0, xw, 1)
    grad_w_x = main_part(xw, xw, 1)
    grad_w_query = main_part(q_at, HEAD_SIZE, 1)
    grad_w_dt = main_part(dt_at, heads, 1)
    out_part = back(grad_w_out, 1)
    grad_out_mamba = out_part(0, xw, 0)
    grad_out_attn = out_part(xw, HEAD_SIZE, 0)
    ffn_part = back(grad_w_ffn, 0)
    grad_w_gate = ffn_part(0, ffn_local, 1)
    grad_w_up = ffn_part(ffn_local, ffn_local, 1)
    grad_w_down = back(grad_w_down, 1)(0, ffn_local, 0)
    grad_w_shared = grad_w_shared.astype(f32)
    kv_width = KEY_VALUE_HEADS * HEAD_SIZE
    grad_w_bc = grad_w_shared[:, :shared_width]
    key_weight_gradient = grad_w_shared[:, shared_width : shared_width + kv_width]
    value_weight_gradient = grad_w_shared[:, shared_width + kv_width :]
    return (
        block_out,
        grad_inputs,
        grad_norm_gain,
        grad_w_z,
        grad_w_x,
        grad_w_dt,
        grad_w_bc,
        grad_conv_x,
        grad_bias_x,
        grad_conv_bc,
        grad_bias_bc,
        grad_dt_bias,
        grad_a_log,
        grad_d_skip,
        grad_mixer_gain,
        grad_out_mamba,
        grad_w_query,
        key_weight_gradient,
        value_weight_gradient,
        grad_out_attn,
        grad_ffn_gain,
        grad_w_gate,
        grad_w_up,
        grad_w_down,
    )


def solution(mesh):
    in_specs = (
        P(("dp", "row"), "col"),
        P(("dp", "row"), "col"),
        P("col"),
        P("col", "row"),
        P("col", "row"),
        P("col", "row"),
        P("col", None),
        P(None, ("row", "col")),
        P(("row", "col")),
        P(),
        P(),
        P(("row", "col")),
        P(("row", "col")),
        P(("row", "col")),
        P(("row", "col")),
        P("row", "col"),
        P("col", "row"),
        P("col", None),
        P("col", None),
        P("row", "col"),
        P("col"),
        P("col", "row"),
        P("col", "row"),
        P("row", "col"),
    )
    out_specs = (
        P(("dp", "row"), "col"),
        P(("dp", "row"), "col"),
        P("col"),
        P("col", "row"),
        P("col", "row"),
        P("col", "row"),
        P("col", None),
        P(None, ("row", "col")),
        P(("row", "col")),
        P(),
        P(),
        P(("row", "col")),
        P(("row", "col")),
        P(("row", "col")),
        P(("row", "col")),
        P("row", "col"),
        P("col", "row"),
        P("col", None),
        P("col", None),
        P("row", "col"),
        P("col"),
        P("col", "row"),
        P("col", "row"),
        P("row", "col"),
    )
    return jax.shard_map(local, mesh=mesh, in_specs=in_specs, out_specs=out_specs, check_vma=False)
```

```python
from functools import partial
import math

import jax
import jax.numpy as jnp
from jax import lax
from jax.experimental import pallas as pl
from jax.experimental.pallas import tpu as pltpu
from jax.sharding import PartitionSpec as P

MODEL_WIDTH = 1024
STATE_SIZE = 128
KC = 4
QUERY_HEADS = 8
KEY_VALUE_HEADS = 2
HEAD_SIZE = 64
CH = 128
QB = 512
DM = 1536


epsilon = 1e-05
rope_base = 100000000000.0
masked_score = -1e30
highest = lax.Precision.HIGHEST


def causal_conv(raw, kernel, offset):
    sequence_length = raw.shape[0]
    padded = jnp.pad(raw, ((KC - 1, 0), (0, 0)))
    summed = offset + kernel[0] * padded[0:sequence_length]
    for tap_index in range(1, KC):
        summed = summed + kernel[tap_index] * padded[tap_index : tap_index + sequence_length]
    return jax.nn.silu(summed)


def apply_rotary(values, token_positions):
    half_width = values.shape[-1] // 2
    frequency = jnp.exp(
        jnp.arange(half_width).astype(jnp.float32) * (-2.0 * math.log(rope_base) / values.shape[-1])
    )
    angle_half = token_positions[:, None] * frequency[None, :]
    angle_full = jnp.concatenate([angle_half, angle_half], axis=-1)[:, None, :]
    turned = jnp.concatenate([-values[..., half_width:], values[..., :half_width]], axis=-1)
    return values * jnp.cos(angle_full) + turned * jnp.sin(angle_full)


ROWS = ((1,), (1,))
COLS = ((0,), (0,))
VMEM_BYTES = 48 * 1024 * 1024


def dot_on(left, right, dims):
    return lax.dot_general(left, right, (dims, ((), ())), preferred_element_type=jnp.float32)


def chunk_masks():
    row = lax.broadcasted_iota(jnp.int32, (CH, CH), 0)
    column = lax.broadcasted_iota(jnp.int32, (CH, CH), 1)
    return row, column


def exact_dot(left, right, dims=((1,), (0,))):
    return lax.dot_general(
        left, right, (dims, ((), ())), precision=highest, preferred_element_type=jnp.float32
    )


def scan_forward_kernel(heads, x_ref, bc_ref, s_ref, a_ref, y_ref, start_ref, state):
    bf16 = jnp.bfloat16

    @pl.when(pl.program_id(0) == 0)
    def _():
        state[...] = jnp.zeros_like(state)

    carry = state[...]
    start_ref[0] = carry
    row, column = chunk_masks()
    causal = row >= column
    lower = jnp.where(causal, 1.0, 0.0)
    steps, decay = s_ref[...], a_ref[...]
    cum = exact_dot(lower, decay)
    cum_row = exact_dot(decay, lower, ((0,), (1,)))
    b_part, c_part = bc_ref[:, :STATE_SIZE], bc_ref[:, STATE_SIZE:]
    scores = dot_on(c_part, b_part, ROWS)
    carried = dot_on(c_part, carry.astype(bf16), ROWS)
    x_all = x_ref[...].astype(jnp.float32)
    width = x_all.shape[1] // heads
    outs, tails, ends = [], [], []
    for h in range(heads):
        span = slice(h * width, (h + 1) * width)
        c_h = cum[:, h : h + 1]
        last = cum[CH - 1 : CH, h : h + 1]
        xs = x_all[:, span] * steps[:, h : h + 1]
        within = jnp.exp(jnp.where(causal, c_h - cum_row[h : h + 1, :], masked_score))
        inside = jnp.dot(
            (within * scores).astype(bf16), xs.astype(bf16), preferred_element_type=jnp.float32
        )
        outs.append(inside + jnp.exp(c_h) * carried[:, span])
        tails.append((xs * jnp.exp(last - c_h)).astype(bf16))
        ends.append(jnp.exp(last))
    y_ref[...] = jnp.concatenate(outs, axis=1)
    update = dot_on(jnp.concatenate(tails, axis=1), b_part, COLS)
    for h in range(heads):
        span = slice(h * width, (h + 1) * width)
        state[span, :] = ends[h] * carry[span, :] + update[span, :]


def scan_backward_kernel(
    heads, x_ref, bc_ref, s_ref, a_ref, dy_ref, start_ref, dx_ref, ds_ref, da_ref, dbc_ref, dstate
):
    bf16 = jnp.bfloat16

    @pl.when(pl.program_id(0) == 0)
    def _():
        dstate[...] = jnp.zeros_like(dstate)

    dend = dstate[...]
    start = start_ref[0]
    dend_low, start_low = dend.astype(bf16), start.astype(bf16)
    row, column = chunk_masks()
    causal = row >= column
    strict = row > column
    lower = jnp.where(causal, 1.0, 0.0)
    upper = jnp.where(column >= row, 1.0, 0.0)
    upper_low = upper.astype(bf16)
    steps, decay = s_ref[...], a_ref[...]
    cum = exact_dot(lower, decay)
    cum_row = exact_dot(decay, lower, ((0,), (1,)))
    b_part, c_part = bc_ref[:, :STATE_SIZE], bc_ref[:, STATE_SIZE:]
    scores = dot_on(c_part, b_part, ROWS)
    carried = dot_on(c_part, start_low, ROWS)
    back = dot_on(b_part, dend_low, ROWS)
    x_all = x_ref[...].astype(jnp.float32)
    dy_all = dy_ref[...]
    dy_low = dy_all.astype(bf16)
    width = x_all.shape[1] // heads
    lane = lax.broadcasted_iota(jnp.int32, (CH, 8), 1)
    zero_small = jnp.zeros((CH, 8), jnp.float32)
    heads_q, heads_r, inner, ds_all = zero_small, zero_small, zero_small, zero_small
    dscores = jnp.zeros((CH, CH), jnp.float32)
    dxs_list, dye_list, tail_list, ends = [], [], [], []
    for h in range(heads):
        span = slice(h * width, (h + 1) * width)
        c_h = cum[:, h : h + 1]
        last = cum[CH - 1 : CH, h : h + 1]
        x_h = x_all[:, span]
        xs = x_h * steps[:, h : h + 1]
        dy_h = dy_all[:, span]
        e_cum = jnp.exp(c_h)
        tail = jnp.exp(last - c_h)
        within = jnp.exp(jnp.where(causal, c_h - cum_row[h : h + 1, :], masked_score))
        dmix = dot_on(dy_low[:, span], xs.astype(bf16), ROWS) * within
        dscores = dscores + dmix
        mixing = (within * scores).astype(bf16)
        back_h = tail * back[:, span]
        dxs = dot_on(mixing, dy_low[:, span], COLS) + back_h
        dye = dy_h * e_cum
        spread = jnp.dot(
            upper_low, (dmix * scores).astype(bf16), preferred_element_type=jnp.float32
        )
        end = jnp.exp(last)
        const = end * jnp.sum(
            jnp.sum(start[span, :] * dend[span, :], axis=1, keepdims=True), axis=0, keepdims=True
        )
        own = lane == h
        heads_q = jnp.where(own, jnp.sum(dye * carried[:, span], axis=1, keepdims=True), heads_q)
        heads_r = jnp.where(own, jnp.sum(xs * back_h, axis=1, keepdims=True), heads_r)
        inner = jnp.where(
            own, jnp.sum(jnp.where(strict, spread, 0.0), axis=1, keepdims=True) + const, inner
        )
        ds_all = jnp.where(own, jnp.sum(dxs * x_h, axis=1, keepdims=True), ds_all)
        dxs_list.append(dxs * steps[:, h : h + 1])
        dye_list.append(dye.astype(bf16))
        tail_list.append((xs * tail).astype(bf16))
        ends.append(end)
    dx_ref[...] = jnp.concatenate(dxs_list, axis=1)
    ds_ref[...] = ds_all
    da_ref[...] = (
        inner + exact_dot(upper, heads_q) + exact_dot(jnp.where(strict, 1.0, 0.0), heads_r)
    )
    dye_all = jnp.concatenate(dye_list, axis=1)
    dscores_low = dscores.astype(bf16)
    dbc_ref[:, :STATE_SIZE] = dot_on(dscores_low, c_part, COLS) + jnp.dot(
        jnp.concatenate(tail_list, axis=1), dend_low, preferred_element_type=jnp.float32
    )
    dbc_ref[:, STATE_SIZE:] = jnp.dot(
        dscores_low, b_part, preferred_element_type=jnp.float32
    ) + jnp.dot(dye_all, start_low, preferred_element_type=jnp.float32)
    update = dot_on(dye_all, c_part, COLS)
    for h in range(heads):
        span = slice(h * width, (h + 1) * width)
        dstate[span, :] = ends[h] * dend[span, :] + update[span, :]


def scan_forward(x_low, bc_low, steps, decay, heads):
    length, channels = x_low.shape
    chunks = length // CH
    rows = lambda width: pl.BlockSpec((CH, width), lambda i: (i, 0))
    return pl.pallas_call(
        partial(scan_forward_kernel, heads),
        grid=(chunks,),
        in_specs=[rows(channels), rows(2 * STATE_SIZE), rows(8), rows(8)],
        out_specs=[
            rows(channels),
            pl.BlockSpec((1, channels, STATE_SIZE), lambda i: (i, 0, 0)),
        ],
        out_shape=[
            jax.ShapeDtypeStruct((length, channels), jnp.float32),
            jax.ShapeDtypeStruct((chunks, channels, STATE_SIZE), jnp.float32),
        ],
        scratch_shapes=[pltpu.VMEM((channels, STATE_SIZE), jnp.float32)],
        compiler_params=pltpu.CompilerParams(vmem_limit_bytes=VMEM_BYTES),
        name="scan_forward",
    )(x_low, bc_low, steps, decay)


def scan_backward(x_low, bc_low, steps, decay, grad_out, starts, heads):
    length, channels = x_low.shape
    chunks = length // CH
    rows = lambda width: pl.BlockSpec((CH, width), lambda i: (chunks - 1 - i, 0))
    return pl.pallas_call(
        partial(scan_backward_kernel, heads),
        grid=(chunks,),
        in_specs=[
            rows(channels),
            rows(2 * STATE_SIZE),
            rows(8),
            rows(8),
            rows(channels),
            pl.BlockSpec((1, channels, STATE_SIZE), lambda i: (chunks - 1 - i, 0, 0)),
        ],
        out_specs=[rows(channels), rows(8), rows(8), rows(2 * STATE_SIZE)],
        out_shape=[
            jax.ShapeDtypeStruct((length, channels), jnp.float32),
            jax.ShapeDtypeStruct((length, 8), jnp.float32),
            jax.ShapeDtypeStruct((length, 8), jnp.float32),
            jax.ShapeDtypeStruct((length, 2 * STATE_SIZE), jnp.float32),
        ],
        scratch_shapes=[pltpu.VMEM((channels, STATE_SIZE), jnp.float32)],
        compiler_params=pltpu.CompilerParams(vmem_limit_bytes=VMEM_BYTES),
        name="scan_backward",
    )(x_low, bc_low, steps, decay, grad_out, starts)


AQ = 256


def masked_scores(q_blk, k_part, first):
    scores = dot_on(q_blk * jnp.bfloat16(HEAD_SIZE ** (-0.5)), k_part, ROWS)
    row = lax.broadcasted_iota(jnp.int32, scores.shape, 0) + first
    column = lax.broadcasted_iota(jnp.int32, scores.shape, 1)
    return jnp.where(column <= row, scores, masked_score)


def attend_forward_kernel(blocks, q_ref, k_ref, v_ref, o_ref, lse_ref):
    for index in range(blocks):

        @pl.when(pl.program_id(0) == index)
        def _(index=index):
            extent = (index + 1) * AQ
            scores = masked_scores(q_ref[...], k_ref[:extent, :], index * AQ)
            peak = jnp.max(scores, axis=1, keepdims=True)
            shifted = jnp.exp(scores - peak)
            total = jnp.sum(shifted, axis=1, keepdims=True)
            out = jnp.dot(
                shifted.astype(jnp.bfloat16), v_ref[:extent, :], preferred_element_type=jnp.float32
            )
            o_ref[...] = (out / total).astype(jnp.bfloat16)
            lse_ref[...] = peak + jnp.log(total)


def attend_backward_kernel(
    blocks, q_ref, k_ref, v_ref, g_ref, lse_ref, dq_ref, dk_ref, dv_ref
):
    scale = HEAD_SIZE ** (-0.5)

    @pl.when(pl.program_id(0) == 0)
    def _():
        dk_ref[...] = jnp.zeros_like(dk_ref)
        dv_ref[...] = jnp.zeros_like(dv_ref)

    for index in range(blocks):

        @pl.when(pl.program_id(0) == index)
        def _(index=index):
            extent = (index + 1) * AQ
            q_blk, g_blk = q_ref[...], g_ref[...]
            k_part, v_part = k_ref[:extent, :], v_ref[:extent, :]
            scores = masked_scores(q_blk, k_part, index * AQ)
            probs = jnp.exp(scores - lse_ref[...])
            grad_probs = dot_on(g_blk, v_part, ROWS)
            centre = jnp.sum(probs * grad_probs, axis=1, keepdims=True)
            grad_scores = (probs * (grad_probs - centre)).astype(jnp.bfloat16)
            dq_ref[...] = (
                jnp.dot(grad_scores, k_part, preferred_element_type=jnp.float32) * scale
            )
            dk_ref[:extent, :] += dot_on(grad_scores, q_blk, COLS) * scale
            dv_ref[:extent, :] += dot_on(probs.astype(jnp.bfloat16), g_blk, COLS)


def attend_forward(queries, key_rows, value_input):
    length = queries.shape[0]
    blocks = length // AQ
    whole = pl.BlockSpec((length, HEAD_SIZE), lambda i: (0, 0))
    part = lambda width: pl.BlockSpec((AQ, width), lambda i: (i, 0))
    return pl.pallas_call(
        partial(attend_forward_kernel, blocks),
        grid=(blocks,),
        in_specs=[part(HEAD_SIZE), whole, whole],
        out_specs=[part(HEAD_SIZE), part(1)],
        out_shape=[
            jax.ShapeDtypeStruct((length, HEAD_SIZE), jnp.bfloat16),
            jax.ShapeDtypeStruct((length, 1), jnp.float32),
        ],
        compiler_params=pltpu.CompilerParams(vmem_limit_bytes=VMEM_BYTES),
        name="attend_forward",
    )(queries, key_rows, value_input)


def attend_backward(queries, key_rows, value_input, grad_low, log_totals):
    length = queries.shape[0]
    blocks = length // AQ
    whole = pl.BlockSpec((length, HEAD_SIZE), lambda i: (0, 0))
    part = lambda width: pl.BlockSpec((AQ, width), lambda i: (i, 0))
    shape = jax.ShapeDtypeStruct((length, HEAD_SIZE), jnp.float32)
    return pl.pallas_call(
        partial(attend_backward_kernel, blocks),
        grid=(blocks,),
        in_specs=[part(HEAD_SIZE), whole, whole, part(HEAD_SIZE), part(1)],
        out_specs=[part(HEAD_SIZE), whole, whole],
        out_shape=[shape, shape, shape],
        compiler_params=pltpu.CompilerParams(vmem_limit_bytes=VMEM_BYTES),
        name="attend_backward",
    )(queries, key_rows, value_input, grad_low, log_totals)


def silu_slope(values):
    sigmoid = jax.nn.sigmoid(values)
    return sigmoid * (1.0 + values * (1.0 - sigmoid))


GRID = ("row", "col")


def swap(values):
    return lax.ppermute(values, "col", [(0, 1), (1, 0)])


def mine(values, axis):
    size = values.shape[axis] // lax.axis_size("col")
    return lax.dynamic_slice_in_dim(values, lax.axis_index("col") * size, size, axis)


def other(values, axis):
    size = values.shape[axis] // lax.axis_size("col")
    return lax.dynamic_slice_in_dim(values, (1 - lax.axis_index("col")) * size, size, axis)


def ordered(own, received, axis):
    first = lax.axis_index("col") == 0
    return jnp.concatenate(
        [jnp.where(first, own, received), jnp.where(first, received, own)], axis=axis
    )


def exchange(values, split_axis, join_axis):
    return ordered(mine(values, split_axis), swap(other(values, split_axis)), join_axis)


def gather_tokens(values):
    return lax.all_gather(values, GRID, axis=0, tiled=True)


def scatter_tokens(values):
    return lax.psum_scatter(
        values.astype(jnp.bfloat16), GRID, scatter_dimension=0, tiled=True
    ).astype(jnp.float32)


def grid_total(values):
    return lax.psum(values, GRID)


def norm_forward(values, gain):
    squares = jnp.sum(values * values, axis=-1)
    scale_row = lax.rsqrt(squares / MODEL_WIDTH + epsilon)
    return (values * scale_row[:, None] * gain, scale_row)


def norm_backward(values, scale_row, gain, grad_out):
    weighted = gain * grad_out
    inner_sum = jnp.sum(weighted * values, axis=-1)
    grad_in = (
        scale_row[:, None] * weighted - values * (scale_row**3 * inner_sum / MODEL_WIDTH)[:, None]
    )
    return (grad_in, jnp.sum(grad_out * values * scale_row[:, None], axis=0))


def dp_total(values):
    return lax.psum(values.astype(jnp.bfloat16), "dp")


def local(
    inputs,
    cotangent,
    norm_gain,
    w_z,
    w_x,
    w_dt,
    w_bc,
    conv_x,
    bias_x,
    conv_bc,
    bias_bc,
    dt_bias,
    a_log,
    d_skip,
    mixer_gain,
    out_mamba,
    w_query,
    key_matrix,
    value_matrix,
    out_attn,
    ffn_gain,
    w_gate,
    w_up,
    w_down,
):
    col_count = lax.axis_size("col")
    row_count = lax.axis_size("row")
    device_position = lax.axis_index("row") * col_count + lax.axis_index("col")
    sequence_length = inputs.shape[0] * row_count
    xw = conv_x.shape[1]
    heads = dt_bias.shape[0]
    ffn_local = w_down.shape[0] // col_count
    f32 = jnp.float32
    bf16 = jnp.bfloat16
    q_at, dt_at, s_at = 2 * xw, 2 * xw + HEAD_SIZE, 2 * xw + 2 * HEAD_SIZE

    x_float = exchange(inputs, 0, 1).astype(f32)
    pad = jnp.zeros((w_dt.shape[0], HEAD_SIZE - heads), bf16)
    sliced = [w_z, w_x, w_query, w_dt]
    shared = jnp.concatenate([w_bc, key_matrix, value_matrix], axis=1)
    own_in = jnp.concatenate([mine(w, 1) for w in sliced] + [pad, shared], axis=1)
    sent_in = jnp.concatenate([other(w, 1) for w in sliced] + [pad, shared], axis=1)
    w_all = ordered(own_in, swap(sent_in), 0)
    gains = jnp.stack([norm_gain, ffn_gain])
    gains = ordered(gains, swap(gains), 1)
    norm_gain, ffn_gain = gains[0], gains[1]
    key_value_head = device_position // (QUERY_HEADS // KEY_VALUE_HEADS)
    kv_at = s_at + 2 * STATE_SIZE
    key_at = kv_at + key_value_head * HEAD_SIZE
    value_at = key_at + KEY_VALUE_HEADS * HEAD_SIZE
    w_in = jnp.concatenate(
        [
            w_all[:, :kv_at],
            lax.dynamic_slice_in_dim(w_all, key_at, HEAD_SIZE, 1),
            lax.dynamic_slice_in_dim(w_all, value_at, HEAD_SIZE, 1),
        ],
        axis=1,
    )
    cot_own = exchange(cotangent, 0, 1)

    normed, scale_one = norm_forward(x_float, norm_gain)
    normed_all = gather_tokens(normed.astype(bf16))
    cot_all = gather_tokens(cot_own)
    normed_all, out_mamba, out_attn, w_down, w_gate, w_up = lax.optimization_barrier(
        (normed_all, out_mamba, out_attn, w_down, w_gate, w_up)
    )
    w_out = exchange(
        jnp.concatenate(
            [
                out_mamba.reshape(col_count, xw, -1),
                out_attn.reshape(col_count, HEAD_SIZE, -1),
                w_down.reshape(col_count, ffn_local, -1),
            ],
            axis=1,
        ).reshape(-1, out_mamba.shape[1]),
        0,
        1,
    )
    w_down_own = w_out[xw + HEAD_SIZE :]
    w_out = w_out[: xw + HEAD_SIZE]
    w_ffn = jnp.concatenate([mine(w_gate, 1), mine(w_up, 1)], axis=1)
    w_ffn = ordered(w_ffn, swap(jnp.concatenate([other(w_gate, 1), other(w_up, 1)], axis=1)), 0)
    projected = jnp.dot(normed_all, w_in, preferred_element_type=f32)
    gate_z = projected[:, :xw]
    x_raw = projected[:, xw : 2 * xw]
    q_raw = projected[:, q_at:dt_at]
    dt_raw = projected[:, dt_at : dt_at + heads]
    bc_raw = projected[:, s_at:kv_at]
    key_unrotated = projected[:, kv_at : kv_at + HEAD_SIZE]
    value_reduced = projected[:, kv_at + HEAD_SIZE :].astype(bf16)
    x_conv, x_conv_pull = jax.vjp(causal_conv, x_raw, conv_x.astype(f32), bias_x)
    bc_conv, bc_conv_pull = jax.vjp(causal_conv, bc_raw, conv_bc.astype(f32), bias_bc)
    x_low = x_conv.astype(bf16)
    bc_low = bc_conv.astype(bf16)
    steps = jax.nn.softplus(dt_raw + dt_bias)
    log_decay = -steps * jnp.exp(a_log)
    widen = ((0, 0), (0, 8 - heads))
    steps_wide, decay_wide = jnp.pad(steps, widen), jnp.pad(log_decay, widen)
    scanned, starts = scan_forward(x_low, bc_low, steps_wide, decay_wide, heads)
    head_width = xw // heads
    skip_row = jnp.repeat(d_skip, head_width)
    ssm_out = scanned + skip_row * x_low.astype(f32)
    gated = ssm_out * jax.nn.silu(gate_z)
    mixer_scale = lax.rsqrt(grid_total(jnp.sum(gated * gated, axis=-1)) / DM + epsilon)
    mixed_low = (gated * mixer_scale[:, None] * mixer_gain).astype(bf16)
    token_positions = jnp.arange(sequence_length).astype(f32)
    qk_rot, qk_pull = jax.vjp(
        partial(apply_rotary, token_positions=token_positions),
        jnp.stack([q_raw, key_unrotated], axis=1),
    )
    q_low = qk_rot[:, 0].astype(bf16)
    k_low = qk_rot[:, 1].astype(bf16)
    attn_low, log_totals = attend_forward(q_low, k_low, value_reduced)
    joined = jnp.concatenate([mixed_low, attn_low], axis=1)
    middle = x_float + scatter_tokens(jnp.dot(joined, w_out, preferred_element_type=f32))
    normed_ffn, scale_two = norm_forward(middle, ffn_gain)
    ffn_all = gather_tokens(normed_ffn.astype(bf16))
    gate_up = jnp.dot(ffn_all, w_ffn, preferred_element_type=f32)
    gate_ffn = gate_up[:, :ffn_local]
    up_ffn = gate_up[:, ffn_local:]
    gate_silu = jax.nn.silu(gate_ffn)
    act = (gate_silu * up_ffn).astype(bf16)
    grad_act = dot_on(cot_all, w_down_own, ROWS)
    grad_gate = grad_act * up_ffn * silu_slope(gate_ffn)
    grad_up = grad_act * gate_silu
    grad_ffn = jnp.concatenate([grad_gate, grad_up], axis=1).astype(bf16)
    grad_ffn_in = scatter_tokens(dot_on(grad_ffn, w_ffn, ROWS))
    block_out = middle + scatter_tokens(jnp.dot(act, w_down_own, preferred_element_type=f32))
    block_out = exchange(block_out.astype(bf16), 1, 0)
    grad_middle_norm, grad_ffn_gain = norm_backward(middle, scale_two, ffn_gain, grad_ffn_in)
    grad_middle = cot_own.astype(f32) + grad_middle_norm
    grad_branch_all = gather_tokens(grad_middle.astype(bf16))
    grad_w_ffn = dp_total(dot_on(ffn_all, grad_ffn, COLS))
    grad_w_down = dp_total(dot_on(act, cot_all, COLS))
    grad_w_out = dp_total(dot_on(joined, grad_branch_all, COLS))
    grad_joined = dot_on(grad_branch_all, w_out, ROWS)
    grad_mixed = grad_joined[:, :xw]
    grad_attn = grad_joined[:, xw:].astype(bf16)
    weighted = mixer_gain * grad_mixed
    inner_sum = grid_total(jnp.sum(weighted * gated, axis=-1))
    grad_q_rot, grad_k_rot, value_gradient = attend_backward(
        q_low, k_low, value_reduced, grad_attn, log_totals
    )
    grad_qk = qk_pull(jnp.stack([grad_q_rot, grad_k_rot], axis=1))[0]
    grad_gated = (
        mixer_scale[:, None] * weighted - gated * (mixer_scale**3 * inner_sum / DM)[:, None]
    )
    grad_mixer_gain = jnp.sum(grad_mixed * gated * mixer_scale[:, None], axis=0)
    grad_ssm = grad_gated * jax.nn.silu(gate_z)
    grad_z = grad_gated * ssm_out * silu_slope(gate_z)
    grad_x_scan, grad_steps, grad_decay, grad_bc = scan_backward(
        x_low, bc_low, steps_wide, decay_wide, grad_ssm, starts, heads
    )
    grad_xc = grad_x_scan + skip_row * grad_ssm
    grad_d_skip = jnp.sum(
        jnp.sum(grad_ssm * x_low.astype(f32), axis=0).reshape(heads, head_width), axis=1
    )
    grad_decay = grad_decay[:, :heads]
    grad_dt = (grad_steps[:, :heads] - grad_decay * jnp.exp(a_log)) * jax.nn.sigmoid(
        dt_raw + dt_bias
    )
    grad_dt_bias = jnp.sum(grad_dt, axis=0)
    grad_a_log = jnp.sum(grad_decay * log_decay, axis=0)
    grad_x_raw, grad_conv_x, grad_bias_x = x_conv_pull(grad_xc)
    grad_bc_raw, grad_conv_bc, grad_bias_bc = bc_conv_pull(grad_bc)
    grad_in = jnp.concatenate(
        [
            grad_z,
            grad_x_raw,
            grad_qk[:, 0],
            grad_dt,
            jnp.zeros((sequence_length, HEAD_SIZE - heads), f32),
            grad_bc_raw,
            grad_qk[:, 1],
            value_gradient,
        ],
        axis=1,
    ).astype(bf16)
    grad_in, grad_w_ffn, grad_w_down, grad_w_out = lax.optimization_barrier(
        (grad_in, grad_w_ffn, grad_w_down, grad_w_out)
    )
    grad_normed = scatter_tokens(dot_on(grad_in, w_in, ROWS))
    grad_w_in = dot_on(normed_all, grad_in, COLS)
    head_selection = (jnp.arange(KEY_VALUE_HEADS) == key_value_head).astype(f32)

    def per_head(values):
        return (head_selection[None, :, None] * values[:, None, :]).reshape(values.shape[0], -1)

    grad_w_shared = jnp.concatenate(
        [
            grad_w_in[:, s_at:kv_at],
            per_head(grad_w_in[:, kv_at : kv_at + HEAD_SIZE]),
            per_head(grad_w_in[:, kv_at + HEAD_SIZE :]),
        ],
        axis=1,
    )
    grad_w_shared = lax.psum_scatter(
        grad_w_shared.astype(bf16), ("col", "row"), scatter_dimension=0, tiled=True
    )
    grad_w_main = dp_total(grad_w_in[:, :s_at])
    grad_w_shared = lax.all_gather(lax.psum(grad_w_shared, "dp"), "row", axis=0, tiled=True)
    grad_x_norm, grad_norm_gain = norm_backward(x_float, scale_one, norm_gain, grad_normed)
    grad_inputs = exchange((grad_middle + grad_x_norm).astype(bf16), 1, 0).astype(f32)

    slot = jnp.concatenate(
        [
            grad_conv_x.reshape(-1),
            grad_bias_x,
            grad_mixer_gain,
            grad_dt_bias,
            grad_a_log,
            grad_d_skip,
        ]
    )
    common = jnp.concatenate(
        [grad_conv_bc.reshape(-1), grad_bias_bc, grad_norm_gain, grad_ffn_gain]
    )
    slot = dp_total(slot).astype(f32)
    small = lax.psum(common, ("dp", "row", "col"))
    conv_end = KC * xw
    grad_conv_x = slot[:conv_end].reshape(KC, xw)
    grad_bias_x = slot[conv_end : conv_end + xw]
    grad_mixer_gain = slot[conv_end + xw : conv_end + 2 * xw]
    tail = slot[conv_end + 2 * xw :]
    grad_dt_bias, grad_a_log, grad_d_skip = tail[:heads], tail[heads : 2 * heads], tail[2 * heads :]
    shared_width = 2 * STATE_SIZE
    grad_conv_bc = small[: KC * shared_width].reshape(KC, shared_width)
    at = KC * shared_width
    grad_bias_bc = small[at : at + shared_width]
    at = at + shared_width
    grad_norm_gain = mine(small[at : at + MODEL_WIDTH], 0)
    grad_ffn_gain = mine(small[at + MODEL_WIDTH : at + 2 * MODEL_WIDTH], 0)

    def back(values, axis):
        own, received = mine(values, axis), swap(other(values, axis))
        first = lax.axis_index("col") == 0
        left = jnp.where(first, own, received).astype(f32)
        right = jnp.where(first, received, own).astype(f32)

        def part(start, size, along):
            return jnp.concatenate(
                [lax.slice_in_dim(v, start, start + size, axis=along) for v in (left, right)],
                axis=along,
            )

        return part

    main_part = back(grad_w_main, 0)
    grad_w_z = main_part(0, xw, 1)
    grad_w_x = main_part(xw, xw, 1)
    grad_w_query = main_part(q_at, HEAD_SIZE, 1)
    grad_w_dt = main_part(dt_at, heads, 1)
    out_part = back(grad_w_out, 1)
    grad_out_mamba = out_part(0, xw, 0)
    grad_out_attn = out_part(xw, HEAD_SIZE, 0)
    ffn_part = back(grad_w_ffn, 0)
    grad_w_gate = ffn_part(0, ffn_local, 1)
    grad_w_up = ffn_part(ffn_local, ffn_local, 1)
    grad_w_down = back(grad_w_down, 1)(0, ffn_local, 0)
    grad_w_shared = grad_w_shared.astype(f32)
    kv_width = KEY_VALUE_HEADS * HEAD_SIZE
    grad_w_bc = grad_w_shared[:, :shared_width]
    key_weight_gradient = grad_w_shared[:, shared_width : shared_width + kv_width]
    value_weight_gradient = grad_w_shared[:, shared_width + kv_width :]
    return (
        block_out,
        grad_inputs,
        grad_norm_gain,
        grad_w_z,
        grad_w_x,
        grad_w_dt,
        grad_w_bc,
        grad_conv_x,
        grad_bias_x,
        grad_conv_bc,
        grad_bias_bc,
        grad_dt_bias,
        grad_a_log,
        grad_d_skip,
        grad_mixer_gain,
        grad_out_mamba,
        grad_w_query,
        key_weight_gradient,
        value_weight_gradient,
        grad_out_attn,
        grad_ffn_gain,
        grad_w_gate,
        grad_w_up,
        grad_w_down,
    )


def solution(mesh):
    in_specs = (
        P(("dp", "row"), "col"),
        P(("dp", "row"), "col"),
        P("col"),
        P("col", "row"),
        P("col", "row"),
        P("col", "row"),
        P("col", None),
        P(None, ("row", "col")),
        P(("row", "col")),
        P(),
        P(),
        P(("row", "col")),
        P(("row", "col")),
        P(("row", "col")),
        P(("row", "col")),
        P("row", "col"),
        P("col", "row"),
        P("col", None),
        P("col", None),
        P("row", "col"),
        P("col"),
        P("col", "row"),
        P("col", "row"),
        P("row", "col"),
    )
    out_specs = (
        P(("dp", "row"), "col"),
        P(("dp", "row"), "col"),
        P("col"),
        P("col", "row"),
        P("col", "row"),
        P("col", "row"),
        P("col", None),
        P(None, ("row", "col")),
        P(("row", "col")),
        P(),
        P(),
        P(("row", "col")),
        P(("row", "col")),
        P(("row", "col")),
        P(("row", "col")),
        P("row", "col"),
        P("col", "row"),
        P("col", None),
        P("col", None),
        P("row", "col"),
        P("col"),
        P("col", "row"),
        P("col", "row"),
        P("row", "col"),
    )
    return jax.shard_map(local, mesh=mesh, in_specs=in_specs, out_specs=out_specs, check_vma=False)
```
